256 devices in a mesh: rep: 16 (over x_lo, y, core), tp: 16 (over x_hi, z).
Axes of the slice: x: 4 (x_hi: 2, x_lo: 2; x = x_hi * 2 + x_lo), y: 4, z: 8, core: 2. Of those that a mesh axis runs over, the one named last changes fastest.
Arguments:
- hidden: bfloat16 [16, 768, 6912], P('rep', None, 'tp'), may hold values from -6 to 6
- residual: bfloat16 [16, 768, 5120], P('rep', 'tp'), may hold values from -6 to 6
- cotangent: bfloat16 [16, 768, 5120], P('rep', 'tp'), may hold values from -6 to 6
- down_state: bfloat16 [16, 6912, 5120], P('rep', 'tp'), may hold values from -6 to 6
- gain_state: bfloat16 [16, 5120], P('rep'), may hold values from 0.5 to 1.5
- push_weight: bfloat16 [16], P('rep'), may hold values from 0.5 to 2
- exponent: int32 [1], replicated, may hold values from 0 to 63
Outputs:
- normed: bfloat16 [16, 768, 5120], P('rep', 'tp')
- new_down: bfloat16 [16, 6912, 5120], P('rep', 'tp')
- new_gain: bfloat16 [16, 5120], P('rep')
- new_weight: float32 [16], P('rep')
The draws below stay inside these ranges and needn't reach their ends.
Inputs may be any that keep to these rules, and one draw needn't show every extreme that they name: Each replica receives from the replica 2 ** (exponent mod min(4, 4)) places behind it on the loop of 16.
All inputs are finite; a program needn't handle non-finite values.
Results may differ from the reference program's by a relative error of at most 0.017.
Values may be sent and summed in bfloat16 or wider, within the bound.
No kernel may reach another device: no remote copies, remote signals or barrier semaphores. Data moves between devices by JAX's collectives and lax.ppermute only.
A program may use at most 128 MiB of HBM per device.

```python
import math
import jax
import jax.numpy as jnp
from jax import lax

D = 5120
FF = 6912
TOK = 768
REPS = 16
N_TP = 16


def base_field(key):
    return jax.random.normal(key, (REPS, TOK, D), jnp.float32)


def draw_residual(key, part):
    base = base_field(key)
    field = base
    return jnp.clip(field, -6.0, 6.0).astype(jnp.bfloat16)


def draw_cotangent(key, part):
    base = base_field(key)
    key = jax.random.fold_in(key, 23)
    sign_key, noise_key = jax.random.split(key)
    signs = jnp.where(jax.random.bernoulli(sign_key, 0.5, (REPS, TOK, 1)), 1.0, -1.0).astype(jnp.float32)
    noise = jax.random.normal(noise_key, (REPS, TOK, D), jnp.float32)
    field = 0.6 * signs * base + 0.8 * noise
    return jnp.clip(field, -6.0, 6.0).astype(jnp.bfloat16)


def block_levels(stream_key, extent, pieces, smallest, high):
    def one(dim, shards_of):
        draws = jax.random.uniform(jax.random.fold_in(jax.random.fold_in(stream_key, 6), dim), (shards_of,), jnp.float32, smallest / len(pieces), high / len(pieces))
        return jnp.repeat(jnp.exp(draws), extent[dim] // shards_of).reshape((-1,) + (1,) * (len(extent) - dim - 1))

    gain = one(*pieces[0])
    for cut in pieces[1:]:
        gain = gain * one(*cut)
    return gain


def gaussian(own_key, extent, width, reach, cuts=(), kind=jnp.bfloat16):
    result = width * jax.random.normal(own_key, extent, jnp.float32)
    if cuts:
        result = result * block_levels(own_key, extent, cuts, -0.22, 0.18)
    return jnp.clip(result, -reach, reach).astype(kind)


def setup_inputs(seed: int = 0) -> dict:
    keys = jax.random.split(jax.random.key(seed), 8)
    return {
        "hidden": gaussian(keys[0], (REPS, TOK, FF), 1.0, 6.0, ((0, 16), (2, 16))),
        "residual": draw_residual(jax.random.fold_in(keys[7], 71), 0),
        "cotangent": draw_cotangent(jax.random.fold_in(keys[7], 71), 0),
        "down_state": gaussian(keys[3], (REPS, FF, D), 1.0, 6.0, ((0, 16), (1, 16))),
        "gain_state": jnp.clip(1.0 + 0.1 * jax.random.normal(keys[4], (REPS, D), jnp.float32), 0.5, 1.5).astype(jnp.bfloat16),
        "push_weight": jnp.clip(jnp.exp(math.log(2.0) - 1.3862944 * jax.random.uniform(keys[5], (REPS,), jnp.float32) ** block_levels(keys[5], (REPS,), ((0, 16),), -0.2, 0.2)), 0.5, 2.0).astype(jnp.bfloat16),
        "exponent": jax.random.randint(keys[6], (1,), 0, 64).astype(jnp.int32),
    }


EPSILON = 1e-05

def replica_step(operands):
    hidden_rows, residual_rows, cotangent_rows, down_rows, gain_row, push_value = operands
    weight_value = push_value.astype(jnp.float32)
    debiased = (down_rows.astype(jnp.float32) / weight_value).astype(jnp.bfloat16)
    fan_scale = 1.0 / math.sqrt(FF)
    group_width = FF // N_TP

    def add_group(group, running):
        offset = (group * group_width).astype(jnp.int32)
        left = lax.dynamic_slice_in_dim(hidden_rows, offset, group_width, 1)
        right = lax.dynamic_slice_in_dim(debiased, offset, group_width, 0)
        rounded = (jnp.dot(left, right, preferred_element_type=jnp.float32) * fan_scale).astype(jnp.bfloat16)
        rounded = lax.optimization_barrier(rounded)
        return running + rounded.astype(jnp.float32)
    branch = lax.fori_loop(jnp.int32(0), jnp.int32(N_TP), add_group, jnp.zeros((TOK, D), jnp.float32))
    summed = residual_rows.astype(jnp.float32) + branch
    inv_rms = lax.rsqrt(lax.optimization_barrier(jnp.mean(summed * summed, axis=-1, keepdims=True)) + EPSILON)
    eff_gain = gain_row.astype(jnp.float32) / weight_value
    normalized = summed * inv_rms
    normed = (normalized * eff_gain).astype(jnp.bfloat16)
    cotangent_wide = cotangent_rows.astype(jnp.float32)
    gain_slope = lax.optimization_barrier(jnp.sum(cotangent_wide * normalized, axis=0))
    scaled = cotangent_wide * eff_gain
    slope_rows = (inv_rms * (scaled - normalized * lax.optimization_barrier(jnp.mean(scaled * normalized, axis=-1, keepdims=True)))).astype(jnp.bfloat16)
    down_slope = jnp.dot(hidden_rows.T, slope_rows, preferred_element_type=jnp.float32) * fan_scale
    down_step = (down_rows.astype(jnp.float32) - 2.0 * down_slope).astype(jnp.bfloat16)
    gain_step = (gain_row.astype(jnp.float32) - 0.03 * gain_slope).astype(jnp.bfloat16)
    return (normed, down_step, gain_step)

def reference(hidden, residual, cotangent, down_state, gain_state, push_weight, exponent):
    normed, down_step, gain_step = lax.map(replica_step, (hidden, residual, cotangent, down_state, gain_state, push_weight))
    branch_count = min(REPS // 4, 4)
    reduced = jnp.remainder(exponent[0].astype(jnp.int32), jnp.int32(branch_count))
    distance = jnp.left_shift(jnp.int32(1), reduced)
    moved_down = jnp.roll(down_step, distance, axis=0)
    moved_gain = jnp.roll(gain_step, distance, axis=0)
    moved_weight = jnp.roll(push_weight, distance, axis=0)
    new_down = (0.5 * (down_step.astype(jnp.float32) + moved_down.astype(jnp.float32))).astype(jnp.bfloat16)
    new_gain = (0.5 * (gain_step.astype(jnp.float32) + moved_gain.astype(jnp.float32))).astype(jnp.bfloat16)
    new_weight = 0.5 * (push_weight.astype(jnp.float32) + moved_weight.astype(jnp.float32))
    return (normed, new_down, new_gain, new_weight)
```

```python
import math

import jax
import jax.numpy as jnp
from jax import lax
from jax.sharding import Mesh
from jax.sharding import PartitionSpec as P

FF = 6912
EPSILON = 1e-05
NX, NZ = 2, 8


def across_x(block):
    return lax.ppermute(block, "x", [(0, 1), (1, 0)])


def sum_over_tp(part):
    part = part + across_x(part)
    for bit in (1, 2, 4):
        part = part + lax.ppermute(part, "z", [(k, k ^ bit) for k in range(NZ)])
    return part


def from_behind(values, reduced):
    def shifted(by):
        return lambda *v: lax.ppermute(v, "rep", [(i, (i + by) % 16) for i in range(16)])

    return lax.switch(reduced, [shifted(by) for by in (1, 2, 4, 8)], *values)


def mixed(mine, moved):
    return 0.5 * (mine.astype(jnp.float32) + moved.astype(jnp.float32))


def per_device(hidden, residual, cotangent, down_state, gain_state, push_weight, exponent):
    fan_scale = 1.0 / math.sqrt(FF)
    x = lax.axis_index("x")
    reduced = jnp.remainder(exponent[0], 4)
    weight_value = push_weight[0].astype(jnp.float32)
    down = down_state[0]
    width = down.shape[1]
    split = hidden[0].reshape(NX, NZ, 48, -1)
    own = lax.dynamic_index_in_dim(split, x, 0, False)
    other = lax.dynamic_index_in_dim(split, 1 - x, 0, False)
    rows = jnp.concatenate([own, other], axis=1).reshape(NZ * NX * 48, -1)
    own = own.reshape(NZ * 48, -1)
    other = other.reshape(NZ * 48, -1)
    factor = fan_scale / weight_value

    def product(lhs, cols):
        wide = jnp.dot(lhs, down[:, cols], preferred_element_type=jnp.float32)
        return (wide * factor).astype(jnp.bfloat16)

    def sum_over_z(terms):
        return lax.psum_scatter(terms, "z", scatter_dimension=0, tiled=True)

    half = width // 2
    low, high = slice(0, half), slice(half, width)
    swapped = across_x(product(other, high))
    low_rows, own = lax.optimization_barrier((rows, own))
    low_sum = sum_over_z(product(low_rows, low))
    high_terms = (product(own, high).astype(jnp.float32) + swapped.astype(jnp.float32)).astype(jnp.bfloat16)
    high_sum = sum_over_z(high_terms).astype(jnp.float32)
    low_sum = low_sum[:48].astype(jnp.float32) + across_x(low_sum[48:]).astype(jnp.float32)
    branch = jnp.concatenate([low_sum, high_sum], axis=1)

    summed = residual[0].astype(jnp.float32) + branch
    inv_rms = lax.rsqrt(jnp.mean(summed * summed, axis=-1, keepdims=True) + EPSILON)
    eff_gain = gain_state[0].astype(jnp.float32) / weight_value
    normalized = summed * inv_rms
    normed = (normalized * eff_gain).astype(jnp.bfloat16)
    cotangent_wide = cotangent[0].astype(jnp.float32)
    gain_part = jnp.sum(cotangent_wide * normalized, axis=0)
    scaled = cotangent_wide * eff_gain
    slope_rows = (
        inv_rms * (scaled - normalized * jnp.mean(scaled * normalized, axis=-1, keepdims=True))
    ).astype(jnp.bfloat16)

    def gathered(mine):
        return lax.all_gather(
            jnp.concatenate([mine, across_x(mine)]), "z", axis=0, tiled=True
        )

    def down_step(block, cols):
        down_slope = (
            lax.dot_general(
                rows, block, (((0,), (0,)), ((), ())), preferred_element_type=jnp.float32
            )
            * fan_scale
        )
        return (down[:, cols].astype(jnp.float32) - 2.0 * down_slope).astype(jnp.bfloat16)

    gain_slope = sum_over_tp(gain_part.reshape(-1, 128)).reshape(-1)
    gain_step = (gain_state[0].astype(jnp.float32) - 0.03 * gain_slope).astype(jnp.bfloat16)
    low_block = gathered(slope_rows[:, low])
    high_block = gathered(slope_rows[:, high])
    low_step = down_step(low_block, low)
    moved_low, moved_gain, moved_weight = from_behind((low_step, gain_step, push_weight), reduced)
    high_step = down_step(high_block, high)
    (moved_high,) = from_behind((high_step,), reduced)
    new_down = jnp.concatenate(
        [
            mixed(low_step, moved_low).astype(jnp.bfloat16),
            mixed(high_step, moved_high).astype(jnp.bfloat16),
        ],
        axis=1,
    )
    new_gain = mixed(gain_step, moved_gain).astype(jnp.bfloat16)
    new_weight = mixed(push_weight, moved_weight)
    return normed[None], new_down[None], new_gain[None], new_weight


def solution(mesh):
    tp = ("x", "z")
    return jax.shard_map(
        per_device,
        mesh=Mesh(mesh.devices.reshape(-1, NX, NZ), ("rep", "x", "z")),
        in_specs=(
            P("rep", None, tp),
            P("rep", tp, None),
            P("rep", tp, None),
            P("rep", tp, None),
            P("rep", None),
            P("rep"),
            P(),
        ),
        out_specs=(P("rep", tp, None), P("rep", tp, None), P("rep", None), P("rep")),
        check_vma=False,
    )
```

```python
import math

import jax
import jax.numpy as jnp
from jax import lax
from jax.sharding import Mesh
from jax.sharding import PartitionSpec as P

FF = 6912
EPSILON = 1e-05
NX, NZ = 2, 8


def across_x(block):
    return lax.ppermute(block, "x", [(0, 1), (1, 0)])


def sum_over_tp(part):
    part = part + across_x(part)
    for bit in (1, 2, 4):
        part = part + lax.ppermute(part, "z", [(k, k ^ bit) for k in range(NZ)])
    return part


def from_behind(values, reduced):
    def shifted(by):
        return lambda *v: lax.ppermute(v, "rep", [(i, (i + by) % 16) for i in range(16)])

    return lax.switch(reduced, [shifted(by) for by in (1, 2, 4, 8)], *values)


def mixed(mine, moved):
    return 0.5 * (mine.astype(jnp.float32) + moved.astype(jnp.float32))


def per_device(hidden, residual, cotangent, down_state, gain_state, push_weight, exponent):
    fan_scale = 1.0 / math.sqrt(FF)
    x = lax.axis_index("x")
    reduced = jnp.remainder(exponent[0], 4)
    weight_value = push_weight[0].astype(jnp.float32)
    down = down_state[0]
    width = down.shape[1]
    split = hidden[0].reshape(NX, NZ, 48, -1)
    own = lax.dynamic_index_in_dim(split, x, 0, False)
    other = lax.dynamic_index_in_dim(split, 1 - x, 0, False)
    rows = jnp.concatenate([own, other], axis=1).reshape(NZ * NX * 48, -1)
    own = own.reshape(NZ * 48, -1)
    other = other.reshape(NZ * 48, -1)
    factor = fan_scale / weight_value

    def product(lhs, cols):
        wide = jnp.dot(lhs, down[:, cols], preferred_element_type=jnp.float32)
        return (wide * factor).astype(jnp.bfloat16)

    def sum_over_z(terms):
        return lax.psum_scatter(terms, "z", scatter_dimension=0, tiled=True)

    half = width // 2
    swapped = across_x(product(other, slice(half, width)))
    early = sum_over_z(product(rows, slice(0, half)))
    terms = product(own, slice(half, width))

    cut = width * 13 // 20
    low, high = slice(0, cut), slice(cut, width)
    terms, swapped = lax.optimization_barrier((terms, swapped))
    terms = (terms.astype(jnp.float32) + swapped.astype(jnp.float32)).astype(jnp.bfloat16)
    terms, early, ahead = lax.optimization_barrier((terms, early, down[:, high]))
    late = sum_over_z(terms)
    (behind_down,) = from_behind((ahead,), reduced)
    late, behind_down = lax.optimization_barrier((late, behind_down))
    early = early[:48].astype(jnp.float32) + across_x(early[48:]).astype(jnp.float32)
    branch = jnp.concatenate([early, late.astype(jnp.float32)], axis=1)

    summed = residual[0].astype(jnp.float32) + branch
    inv_rms = lax.rsqrt(jnp.mean(summed * summed, axis=-1, keepdims=True) + EPSILON)
    eff_gain = gain_state[0].astype(jnp.float32) / weight_value
    normalized = summed * inv_rms
    normed = (normalized * eff_gain).astype(jnp.bfloat16)
    cotangent_wide = cotangent[0].astype(jnp.float32)
    gain_part = jnp.sum(cotangent_wide * normalized, axis=0)
    scaled = cotangent_wide * eff_gain
    slope_rows = (
        inv_rms * (scaled - normalized * jnp.mean(scaled * normalized, axis=-1, keepdims=True))
    ).astype(jnp.bfloat16)

    def along_z(block):
        return lax.all_gather(block, "z", axis=0, tiled=True)

    def down_step(state, token_rows, block):
        down_slope = (
            lax.dot_general(
                token_rows, block, (((0,), (0,)), ((), ())), preferred_element_type=jnp.float32
            )
            * fan_scale
        )
        return (state.astype(jnp.float32) - 2.0 * down_slope).astype(jnp.bfloat16)

    low_slope = slope_rows[:, low]
    low_block = along_z(jnp.concatenate([low_slope, across_x(low_slope)]))
    (behind_slope,) = from_behind((slope_rows[:, high],), reduced)
    both = jnp.concatenate([slope_rows[:, high], behind_slope], axis=1)
    both = jnp.concatenate([both, across_x(both)])
    both, ahead = lax.optimization_barrier((both, rows))
    high_block = along_z(both)
    (behind_rows,) = from_behind((ahead,), reduced)
    gain_slope = sum_over_tp(gain_part.reshape(-1, 128)).reshape(-1)
    gain_step = (gain_state[0].astype(jnp.float32) - 0.03 * gain_slope).astype(jnp.bfloat16)
    low_block, behind_rows, gain_step = lax.optimization_barrier((low_block, behind_rows, gain_step))
    low_step = down_step(down[:, low], rows, low_block)
    moved_low, moved_gain, moved_weight = from_behind((low_step, gain_step, push_weight), reduced)
    new_down = jnp.pad(mixed(low_step, moved_low).astype(jnp.bfloat16), ((0, 0), (0, width - cut)))
    new_down, high_block = lax.optimization_barrier((new_down, high_block))
    high_step = down_step(down[:, high], rows, high_block[:, : width - cut])
    behind_step = down_step(behind_down, behind_rows, high_block[:, width - cut :])
    new_down = lax.dynamic_update_slice(
        new_down, mixed(high_step, behind_step).astype(jnp.bfloat16), (0, cut)
    )
    new_gain = mixed(gain_step, moved_gain).astype(jnp.bfloat16)
    new_weight = mixed(push_weight, moved_weight)
    return normed[None], new_down[None], new_gain[None], new_weight


def solution(mesh):
    tp = ("x", "z")
    return jax.shard_map(
        per_device,
        mesh=Mesh(mesh.devices.reshape(-1, NX, NZ), ("rep", "x", "z")),
        in_specs=(
            P("rep", None, tp),
            P("rep", tp, None),
            P("rep", tp, None),
            P("rep", tp, None),
            P("rep", None),
            P("rep"),
            P(),
        ),
        out_specs=(P("rep", tp, None), P("rep", tp, None), P("rep", None), P("rep")),
        check_vma=False,
    )
```

```python
import math

import jax
import jax.numpy as jnp
from jax import lax
from jax.sharding import Mesh
from jax.sharding import PartitionSpec as P

FF = 6912
EPSILON = 1e-05
NX, NZ = 2, 8


def across_x(block):
    return lax.ppermute(block, "x", [(0, 1), (1, 0)])


def sum_over_tp(part):
    part = part + across_x(part)
    for bit in (1, 2, 4):
        part = part + lax.ppermute(part, "z", [(k, k ^ bit) for k in range(NZ)])
    return part


def from_behind(values, reduced):
    def shifted(by):
        return lambda *v: lax.ppermute(v, "rep", [(i, (i + by) % 16) for i in range(16)])

    return lax.switch(reduced, [shifted(by) for by in (1, 2, 4, 8)], *values)


def mixed(mine, moved):
    return 0.5 * (mine.astype(jnp.float32) + moved.astype(jnp.float32))


def per_device(hidden, residual, cotangent, down_state, gain_state, push_weight, exponent):
    fan_scale = 1.0 / math.sqrt(FF)
    x = lax.axis_index("x")
    reduced = jnp.remainder(exponent[0], 4)
    weight_value = push_weight[0].astype(jnp.float32)
    down = down_state[0]
    width = down.shape[1]
    split = hidden[0].reshape(NX, NZ, 48, -1)
    own = lax.dynamic_index_in_dim(split, x, 0, False)
    other = lax.dynamic_index_in_dim(split, 1 - x, 0, False)
    rows = jnp.concatenate([own, other], axis=1).reshape(NZ * NX * 48, -1)
    own = own.reshape(NZ * 48, -1)
    other = other.reshape(NZ * 48, -1)
    factor = fan_scale / weight_value

    def product(lhs, cols):
        wide = jnp.dot(lhs, down[:, cols], preferred_element_type=jnp.float32)
        return (wide * factor).astype(jnp.bfloat16)

    def sum_over_z(terms):
        return lax.psum_scatter(terms, "z", scatter_dimension=0, tiled=True)

    half = width // 2
    swapped = across_x(product(other, slice(half, width)))
    early = sum_over_z(product(rows, slice(0, half)))
    terms = product(own, slice(half, width))

    cut = width * 13 // 20
    low, high = slice(0, cut), slice(cut, width)
    terms, swapped = lax.optimization_barrier((terms, swapped))
    terms = (terms.astype(jnp.float32) + swapped.astype(jnp.float32)).astype(jnp.bfloat16)
    terms, early, ahead = lax.optimization_barrier((terms, early, down[:, high]))
    late = sum_over_z(terms)
    (behind_down,) = from_behind((ahead,), reduced)
    late, behind_down = lax.optimization_barrier((late, behind_down))
    early = early[:48].astype(jnp.float32) + across_x(early[48:]).astype(jnp.float32)
    branch = jnp.concatenate([early, late.astype(jnp.float32)], axis=1)

    summed = residual[0].astype(jnp.float32) + branch
    inv_rms = lax.rsqrt(jnp.mean(summed * summed, axis=-1, keepdims=True) + EPSILON)
    eff_gain = gain_state[0].astype(jnp.float32) / weight_value
    normalized = summed * inv_rms
    normed = (normalized * eff_gain).astype(jnp.bfloat16)
    cotangent_wide = cotangent[0].astype(jnp.float32)
    gain_part = jnp.sum(cotangent_wide * normalized, axis=0)
    scaled = cotangent_wide * eff_gain
    slope_rows = (
        inv_rms * (scaled - normalized * jnp.mean(scaled * normalized, axis=-1, keepdims=True))
    ).astype(jnp.bfloat16)

    def along_z(block):
        return lax.all_gather(block, "z", axis=0, tiled=True)

    def token_sum(token_rows, block):
        return lax.dot_general(
            token_rows, block, (((0,), (0,)), ((), ())), preferred_element_type=jnp.float32
        )

    low_slope = slope_rows[:, low]
    low_block = along_z(jnp.concatenate([low_slope, across_x(low_slope)]))
    (behind_slope,) = from_behind((slope_rows[:, high],), reduced)
    both = jnp.concatenate([slope_rows[:, high], behind_slope])
    both = jnp.concatenate([both, across_x(both)])
    gain_slope = sum_over_tp(gain_part.reshape(-1, 128)).reshape(-1)
    gain_step = (gain_state[0].astype(jnp.float32) - 0.03 * gain_slope).astype(jnp.bfloat16)
    both, ahead, gain_step = lax.optimization_barrier((both, rows, gain_step))
    high_block = along_z(both)
    behind_rows, moved_gain, moved_weight = from_behind((ahead, gain_step, push_weight), reduced)
    new_gain = mixed(gain_step, moved_gain).astype(jnp.bfloat16)
    new_weight = mixed(push_weight, moved_weight)

    stacked = jnp.concatenate(
        [v.reshape(NZ, NX, 1, 48, -1) for v in (rows, behind_rows)], axis=2
    ).reshape(NZ * NX * 2 * 48, -1)
    buffer = -down
    low_block, stacked, new_gain, buffer = lax.optimization_barrier(
        (low_block, stacked, new_gain, buffer)
    )
    low_step = (
        down[:, low].astype(jnp.float32) - 2.0 * fan_scale * token_sum(rows, low_block)
    ).astype(jnp.bfloat16)
    (moved_low,) = from_behind((low_step,), reduced)
    new_down = lax.dynamic_update_slice(
        buffer, mixed(low_step, moved_low).astype(jnp.bfloat16), (0, 0)
    )
    new_down, high_block = lax.optimization_barrier((new_down, high_block))
    new_high = mixed(down[:, high], behind_down) - fan_scale * token_sum(stacked, high_block)
    new_down = lax.dynamic_update_slice(new_down, new_high.astype(jnp.bfloat16), (0, cut))
    return normed[None], new_down[None], new_gain[None], new_weight


def solution(mesh):
    tp = ("x", "z")
    return jax.shard_map(
        per_device,
        mesh=Mesh(mesh.devices.reshape(-1, NX, NZ), ("rep", "x", "z")),
        in_specs=(
            P("rep", None, tp),
            P("rep", tp, None),
            P("rep", tp, None),
            P("rep", tp, None),
            P("rep", None),
            P("rep"),
            P(),
        ),
        out_specs=(P("rep", tp, None), P("rep", tp, None), P("rep", None), P("rep")),
        check_vma=False,
    )
```

```python
import math

import jax
import jax.numpy as jnp
from jax import lax
from jax.experimental import pallas as pl
from jax.experimental.pallas import tpu as pltpu
from jax.sharding import Mesh
from jax.sharding import PartitionSpec as P

FF = 6912
EPSILON = 1e-05
NX, NZ = 2, 8
TILE = 256


def columns(rows, place):
    return pl.BlockSpec((rows, TILE), lambda j: (0, place(j)))


def whole(value):
    return pl.BlockSpec(value.shape, lambda j: (0, 0))


def over_columns(body, tiles, rows, in_specs, flops, *values):
    return pl.pallas_call(
        body,
        grid=(tiles,),
        in_specs=in_specs,
        out_specs=columns(rows, lambda j: j),
        out_shape=jax.ShapeDtypeStruct((rows, tiles * TILE), jnp.bfloat16),
        compiler_params=pltpu.CompilerParams(vmem_limit_bytes=56 * 2**20),
        cost_estimate=pl.CostEstimate(
            flops=flops, bytes_accessed=sum(v.size * v.dtype.itemsize for v in values), transcendentals=0
        ),
    )(*values)


def scaled_product(lhs, rhs, factor, tiles):
    def body(factor_ref, lhs_ref, rhs_ref, out_ref):
        wide = jnp.dot(lhs_ref[...], rhs_ref[...], preferred_element_type=jnp.float32)
        out_ref[...] = (wide * factor_ref[0]).astype(jnp.bfloat16)

    specs = [pl.BlockSpec(memory_space=pltpu.SMEM), whole(lhs), columns(rhs.shape[0], lambda j: j)]
    flops = 2 * lhs.size * tiles * TILE
    return over_columns(body, tiles, lhs.shape[0], specs, flops, factor.reshape(1), lhs, rhs)


def stepped(state, lhs, rhs, scale):
    def body(state_ref, lhs_ref, rhs_ref, out_ref):
        wide = jnp.dot(lhs_ref[...], rhs_ref[...], preferred_element_type=jnp.float32)
        out_ref[...] = (state_ref[...].astype(jnp.float32) - scale * wide).astype(jnp.bfloat16)

    tiles = rhs.shape[1] // TILE
    specs = [columns(state.shape[0], lambda j: j), whole(lhs), columns(rhs.shape[0], lambda j: j)]
    flops = 2 * lhs.size * rhs.shape[1]
    return over_columns(body, tiles, state.shape[0], specs, flops, state, lhs, rhs)


def merged(low_step, moved_low, state, behind_state, lhs, rhs, scale):
    first = low_step.shape[1] // TILE
    tiles = state.shape[1] // TILE

    def body(low_ref, moved_ref, state_ref, behind_ref, lhs_ref, rhs_ref, out_ref):
        @pl.when(pl.program_id(0) < first)
        def _():
            out_ref[...] = mixed(low_ref[...], moved_ref[...]).astype(jnp.bfloat16)

        @pl.when(pl.program_id(0) >= first)
        def _():
            wide = jnp.dot(lhs_ref[...], rhs_ref[...], preferred_element_type=jnp.float32)
            out_ref[...] = (mixed(state_ref[...], behind_ref[...]) - scale * wide).astype(jnp.bfloat16)

    def low(j):
        return jnp.minimum(j, first - 1)

    def high(j):
        return jnp.maximum(j - first, 0)

    rows = state.shape[0]
    specs = [
        columns(rows, low),
        columns(rows, low),
        columns(rows, lambda j: jnp.maximum(j, first)),
        columns(rows, high),
        whole(lhs),
        columns(rhs.shape[0], high),
    ]
    flops = 2 * lhs.size * rhs.shape[1]
    return over_columns(
        body, tiles, rows, specs, flops, low_step, moved_low, state, behind_state, lhs, rhs
    )


def across_x(block):
    return lax.ppermute(block, "x", [(0, 1), (1, 0)])


def sum_over_tp(part):
    part = part + across_x(part)
    for bit in (1, 2, 4):
        part = part + lax.ppermute(part, "z", [(k, k ^ bit) for k in range(NZ)])
    return part


def from_behind(values, reduced):
    def shifted(by):
        return lambda *v: lax.ppermute(v, "rep", [(i, (i + by) % 16) for i in range(16)])

    return lax.switch(reduced, [shifted(by) for by in (1, 2, 4, 8)], *values)


def mixed(mine, moved):
    return 0.5 * (mine.astype(jnp.float32) + moved.astype(jnp.float32))


def per_device(hidden, residual, cotangent, down_state, gain_state, push_weight, exponent):
    fan_scale = 1.0 / math.sqrt(FF)
    x = lax.axis_index("x")
    reduced = jnp.remainder(exponent[0], 4)
    weight_value = push_weight[0].astype(jnp.float32)
    down = down_state[0]
    width = down.shape[1]
    split = hidden[0].reshape(NX, NZ, 48, -1)
    own = lax.dynamic_index_in_dim(split, x, 0, False)
    other = lax.dynamic_index_in_dim(split, 1 - x, 0, False)
    rows = jnp.concatenate([own, other], axis=1).reshape(NZ * NX * 48, -1)
    own = own.reshape(NZ * 48, -1)
    other = other.reshape(NZ * 48, -1)
    factor = fan_scale / weight_value

    def product(lhs, cols):
        wide = jnp.dot(lhs, down[:, cols], preferred_element_type=jnp.float32)
        return (wide * factor).astype(jnp.bfloat16)

    def sum_over_z(terms):
        return lax.psum_scatter(terms, "z", scatter_dimension=0, tiled=True)

    half = width * 9 // 20
    swapped = across_x(product(other, slice(half, width)))
    early = sum_over_z(scaled_product(rows, down, factor, half // TILE))
    terms = product(own, slice(half, width))

    cut = width * 13 // 20
    low, high = slice(0, cut), slice(cut, width)
    terms, swapped = lax.optimization_barrier((terms, swapped))
    terms = (terms.astype(jnp.float32) + swapped.astype(jnp.float32)).astype(jnp.bfloat16)
    terms, early, ahead = lax.optimization_barrier((terms, early, down[:, high]))
    late = sum_over_z(terms)
    (behind_down,) = from_behind((ahead,), reduced)
    late, behind_down = lax.optimization_barrier((late, behind_down))
    early = early[:48].astype(jnp.float32) + across_x(early[48:]).astype(jnp.float32)
    branch = jnp.concatenate([early, late.astype(jnp.float32)], axis=1)

    summed = residual[0].astype(jnp.float32) + branch
    inv_rms = lax.rsqrt(jnp.mean(summed * summed, axis=-1, keepdims=True) + EPSILON)
    eff_gain = gain_state[0].astype(jnp.float32) / weight_value
    normalized = summed * inv_rms
    normed = (normalized * eff_gain).astype(jnp.bfloat16)
    cotangent_wide = cotangent[0].astype(jnp.float32)
    gain_part = jnp.sum(cotangent_wide * normalized, axis=0)
    scaled = cotangent_wide * eff_gain
    slope_rows = (
        inv_rms * (scaled - normalized * jnp.mean(scaled * normalized, axis=-1, keepdims=True))
    ).astype(jnp.bfloat16)

    def along_z(block):
        return lax.all_gather(block, "z", axis=0, tiled=True)

    low_slope = slope_rows[:, low]
    low_block = along_z(jnp.concatenate([low_slope, across_x(low_slope)]))
    (behind_slope,) = from_behind((slope_rows[:, high],), reduced)
    both = jnp.concatenate([slope_rows[:, high], behind_slope])
    both = jnp.concatenate([both, across_x(both)])
    gain_slope = sum_over_tp(gain_part.reshape(-1, 128)).reshape(-1)
    gain_step = (gain_state[0].astype(jnp.float32) - 0.03 * gain_slope).astype(jnp.bfloat16)
    both, ahead, gain_step = lax.optimization_barrier((both, rows, gain_step))
    high_block = along_z(both)
    behind_rows, moved_gain, moved_weight = from_behind((ahead, gain_step, push_weight), reduced)
    new_gain = mixed(gain_step, moved_gain).astype(jnp.bfloat16)
    new_weight = mixed(push_weight, moved_weight)

    stacked = jnp.concatenate(
        [v.reshape(NZ, NX, 1, 48, -1) for v in (rows, behind_rows)], axis=2
    ).reshape(NZ * NX * 2 * 48, -1)
    rows_across, stacked = rows.T, stacked.T
    low_block, rows_across, stacked, new_gain = lax.optimization_barrier(
        (low_block, rows_across, stacked, new_gain)
    )
    low_step = stepped(down, rows_across, low_block, 2.0 * fan_scale)
    (moved_low,) = from_behind((low_step,), reduced)
    new_down = merged(low_step, moved_low, down, behind_down, stacked, high_block, fan_scale)
    return normed[None], new_down[None], new_gain[None], new_weight


def solution(mesh):
    tp = ("x", "z")
    return jax.shard_map(
        per_device,
        mesh=Mesh(mesh.devices.reshape(-1, NX, NZ), ("rep", "x", "z")),
        in_specs=(
            P("rep", None, tp),
            P("rep", tp, None),
            P("rep", tp, None),
            P("rep", tp, None),
            P("rep", None),
            P("rep"),
            P(),
        ),
        out_specs=(P("rep", tp, None), P("rep", tp, None), P("rep", None), P("rep")),
        check_vma=False,
    )
```

```python
import math

import jax
import jax.numpy as jnp
from jax import lax
from jax.sharding import Mesh
from jax.sharding import PartitionSpec as P

FF = 6912
EPSILON = 1e-05
NX, NZ = 2, 8


def across_x(block):
    return lax.ppermute(block, "x", [(0, 1), (1, 0)])


def sum_over_tp(part):
    part = part + across_x(part)
    for bit in (1, 2, 4):
        part = part + lax.ppermute(part, "z", [(k, k ^ bit) for k in range(NZ)])
    return part


def from_behind(values, reduced):
    def shifted(by):
        return lambda *v: lax.ppermute(v, "rep", [(i, (i + by) % 16) for i in range(16)])

    return lax.switch(reduced, [shifted(by) for by in (1, 2, 4, 8)], *values)


def mixed(mine, moved):
    return 0.5 * (mine.astype(jnp.float32) + moved.astype(jnp.float32))


def per_device(hidden, residual, cotangent, down_state, gain_state, push_weight, exponent):
    fan_scale = 1.0 / math.sqrt(FF)
    x = lax.axis_index("x")
    reduced = jnp.remainder(exponent[0], 4)
    weight_value = push_weight[0].astype(jnp.float32)
    down = down_state[0]
    width = down.shape[1]
    split = hidden[0].reshape(NX, NZ, 48, -1)
    own = lax.dynamic_index_in_dim(split, x, 0, False)
    other = lax.dynamic_index_in_dim(split, 1 - x, 0, False)
    rows = jnp.concatenate([own, other], axis=1).reshape(NZ * NX * 48, -1)
    own = own.reshape(NZ * 48, -1)
    other = other.reshape(NZ * 48, -1)
    factor = fan_scale / weight_value

    def product(lhs, cols):
        wide = jnp.dot(lhs, down[:, cols], preferred_element_type=jnp.float32)
        return (wide * factor).astype(jnp.bfloat16)

    def sum_over_z(terms):
        return lax.psum_scatter(terms, "z", scatter_dimension=0, tiled=True)

    half = width // 2
    swapped = across_x(product(other, slice(half, width)))
    early = sum_over_z(product(rows, slice(0, half)))
    terms = product(own, slice(half, width))

    cut = width * 5 // 8
    low, high = slice(0, cut), slice(cut, width)
    terms, swapped = lax.optimization_barrier((terms, swapped))
    terms = (terms.astype(jnp.float32) + swapped.astype(jnp.float32)).astype(jnp.bfloat16)
    terms, early, ahead = lax.optimization_barrier((terms, early, down[:, high]))
    late = sum_over_z(terms)
    (behind_down,) = from_behind((ahead,), reduced)
    late, behind_down = lax.optimization_barrier((late, behind_down))
    early = early[:48].astype(jnp.float32) + across_x(early[48:]).astype(jnp.float32)
    branch = jnp.concatenate([early, late.astype(jnp.float32)], axis=1)

    summed = residual[0].astype(jnp.float32) + branch
    inv_rms = lax.rsqrt(jnp.mean(summed * summed, axis=-1, keepdims=True) + EPSILON)
    eff_gain = gain_state[0].astype(jnp.float32) / weight_value
    normalized = summed * inv_rms
    normed = (normalized * eff_gain).astype(jnp.bfloat16)
    cotangent_wide = cotangent[0].astype(jnp.float32)
    gain_part = jnp.sum(cotangent_wide * normalized, axis=0)
    scaled = cotangent_wide * eff_gain
    slope_rows = (
        inv_rms * (scaled - normalized * jnp.mean(scaled * normalized, axis=-1, keepdims=True))
    ).astype(jnp.bfloat16)

    def along_z(block):
        return lax.all_gather(block, "z", axis=0, tiled=True)

    def token_sum(token_rows, block):
        return lax.dot_general(
            token_rows, block, (((0,), (0,)), ((), ())), preferred_element_type=jnp.float32
        )

    low_slope = slope_rows[:, low]
    low_block = along_z(jnp.concatenate([low_slope, across_x(low_slope)]))
    (behind_slope,) = from_behind((slope_rows[:, high],), reduced)
    both = jnp.concatenate([slope_rows[:, high], behind_slope])
    both = jnp.concatenate([both, across_x(both)])
    gain_slope = sum_over_tp(gain_part.reshape(-1, 128)).reshape(-1)
    gain_step = (gain_state[0].astype(jnp.float32) - 0.03 * gain_slope).astype(jnp.bfloat16)
    both, ahead, gain_step = lax.optimization_barrier((both, rows, gain_step))
    high_block = along_z(both)
    behind_rows, moved_gain, moved_weight = from_behind((ahead, gain_step, push_weight), reduced)
    new_gain = mixed(gain_step, moved_gain).astype(jnp.bfloat16)
    new_weight = mixed(push_weight, moved_weight)

    stacked = jnp.concatenate(
        [v.reshape(NZ, NX, 1, 48, -1) for v in (rows, behind_rows)], axis=2
    ).reshape(NZ * NX * 2 * 48, -1)
    buffer = -down
    low_block, stacked, new_gain, buffer = lax.optimization_barrier(
        (low_block, stacked, new_gain, buffer)
    )
    low_step = (
        down[:, low].astype(jnp.float32) - 2.0 * fan_scale * token_sum(rows, low_block)
    ).astype(jnp.bfloat16)
    (moved_low,) = from_behind((low_step,), reduced)
    new_down = lax.dynamic_update_slice(
        buffer, mixed(low_step, moved_low).astype(jnp.bfloat16), (0, 0)
    )
    new_down, high_block = lax.optimization_barrier((new_down, high_block))
    new_high = mixed(down[:, high], behind_down) - fan_scale * token_sum(stacked, high_block)
    new_down = lax.dynamic_update_slice(new_down, new_high.astype(jnp.bfloat16), (0, cut))
    return normed[None], new_down[None], new_gain[None], new_weight


def solution(mesh):
    tp = ("x", "z")
    return jax.shard_map(
        per_device,
        mesh=Mesh(mesh.devices.reshape(-1, NX, NZ), ("rep", "x", "z")),
        in_specs=(
            P("rep", None, tp),
            P("rep", tp, None),
            P("rep", tp, None),
            P("rep", tp, None),
            P("rep", None),
            P("rep"),
            P(),
        ),
        out_specs=(P("rep", tp, None), P("rep", tp, None), P("rep", None), P("rep")),
        check_vma=False,
    )
```

```python
import math

import jax
import jax.numpy as jnp
from jax import lax
from jax.sharding import Mesh
from jax.sharding import PartitionSpec as P

FF = 6912
EPSILON = 1e-05
NX, NZ = 2, 8


def across_x(block):
    return lax.ppermute(block, "x", [(0, 1), (1, 0)])


def sum_over_tp(part):
    part = part + across_x(part)
    for bit in (1, 2, 4):
        part = part + lax.ppermute(part, "z", [(k, k ^ bit) for k in range(NZ)])
    return part


def from_behind(values, reduced):
    def shifted(by):
        return lambda *v: lax.ppermute(v, "rep", [(i, (i + by) % 16) for i in range(16)])

    return lax.switch(reduced, [shifted(by) for by in (1, 2, 4, 8)], *values)


def mixed(mine, moved):
    return 0.5 * (mine.astype(jnp.float32) + moved.astype(jnp.float32))


def per_device(hidden, residual, cotangent, down_state, gain_state, push_weight, exponent):
    fan_scale = 1.0 / math.sqrt(FF)
    x = lax.axis_index("x")
    reduced = jnp.remainder(exponent[0], 4)
    weight_value = push_weight[0].astype(jnp.float32)
    down = down_state[0]
    width = down.shape[1]
    split = hidden[0].reshape(NX, NZ, 48, -1)
    own = lax.dynamic_index_in_dim(split, x, 0, False)
    other = lax.dynamic_index_in_dim(split, 1 - x, 0, False)
    rows = jnp.concatenate([own, other], axis=1).reshape(NZ * NX * 48, -1)
    own = own.reshape(NZ * 48, -1)
    other = other.reshape(NZ * 48, -1)
    factor = fan_scale / weight_value

    def product(lhs, cols):
        wide = jnp.dot(lhs, down[:, cols], preferred_element_type=jnp.float32)
        return (wide * factor).astype(jnp.bfloat16)

    def sum_over_z(terms):
        return lax.psum_scatter(terms, "z", scatter_dimension=0, tiled=True)

    half = width // 2
    swapped = across_x(product(other, slice(half, width)))
    early = sum_over_z(product(rows, slice(0, half)))
    terms = product(own, slice(half, width))

    cut = width * 13 // 20
    low, high = slice(0, cut), slice(cut, width)
    terms, swapped = lax.optimization_barrier((terms, swapped))
    terms = (terms.astype(jnp.float32) + swapped.astype(jnp.float32)).astype(jnp.bfloat16)
    terms, early, ahead = lax.optimization_barrier((terms, early, down[:, high]))
    late = sum_over_z(terms)
    (behind_down,) = from_behind((ahead,), reduced)
    late, behind_down = lax.optimization_barrier((late, behind_down))
    early = early[:48].astype(jnp.float32) + across_x(early[48:]).astype(jnp.float32)
    branch = jnp.concatenate([early, late.astype(jnp.float32)], axis=1)

    summed = residual[0].astype(jnp.float32) + branch
    inv_rms = lax.rsqrt(jnp.mean(summed * summed, axis=-1, keepdims=True) + EPSILON)
    eff_gain = gain_state[0].astype(jnp.float32) / weight_value
    normalized = summed * inv_rms
    normed = (normalized * eff_gain).astype(jnp.bfloat16)
    cotangent_wide = cotangent[0].astype(jnp.float32)
    gain_part = jnp.sum(cotangent_wide * normalized, axis=0)
    scaled = cotangent_wide * eff_gain
    slope_rows = (
        inv_rms * (scaled - normalized * jnp.mean(scaled * normalized, axis=-1, keepdims=True))
    ).astype(jnp.bfloat16)

    def along_z(block):
        return lax.all_gather(block, "z", axis=0, tiled=True)

    def token_sum(token_rows, block):
        return lax.dot_general(
            token_rows, block, (((0,), (0,)), ((), ())), preferred_element_type=jnp.float32
        )

    low_slope = slope_rows[:, low]
    low_block = along_z(jnp.concatenate([low_slope, across_x(low_slope)]))
    (behind_slope,) = from_behind((slope_rows[:, high],), reduced)
    both = jnp.concatenate([slope_rows[:, high], behind_slope])
    both = jnp.concatenate([both, across_x(both)])
    gain_slope = sum_over_tp(gain_part.reshape(-1, 128)).reshape(-1)
    gain_step = (gain_state[0].astype(jnp.float32) - 0.03 * gain_slope).astype(jnp.bfloat16)
    both, ahead, gain_step = lax.optimization_barrier((both, rows, gain_step))
    high_block = along_z(both)
    behind_rows, moved_gain, moved_weight = from_behind((ahead, gain_step, push_weight), reduced)
    new_gain = mixed(gain_step, moved_gain).astype(jnp.bfloat16)
    new_weight = mixed(push_weight, moved_weight)

    stacked = jnp.concatenate(
        [v.reshape(NZ, NX, 1, 48, -1) for v in (rows, behind_rows)], axis=2
    ).reshape(NZ * NX * 2 * 48, -1)
    low_block, stacked, new_gain = lax.optimization_barrier((low_block, stacked, new_gain))
    low_step = (
        down[:, low].astype(jnp.float32) - 2.0 * fan_scale * token_sum(rows, low_block)
    ).astype(jnp.bfloat16)
    (moved_low,) = from_behind((low_step,), reduced)
    new_down = jnp.pad(mixed(low_step, moved_low).astype(jnp.bfloat16), ((0, 0), (0, width - cut)))
    new_down, high_block = lax.optimization_barrier((new_down, high_block))
    new_high = mixed(down[:, high], behind_down) - fan_scale * token_sum(stacked, high_block)
    new_down = lax.dynamic_update_slice(new_down, new_high.astype(jnp.bfloat16), (0, cut))
    return normed[None], new_down[None], new_gain[None], new_weight


def solution(mesh):
    tp = ("x", "z")
    return jax.shard_map(
        per_device,
        mesh=Mesh(mesh.devices.reshape(-1, NX, NZ), ("rep", "x", "z")),
        in_specs=(
            P("rep", None, tp),
            P("rep", tp, None),
            P("rep", tp, None),
            P("rep", tp, None),
            P("rep", None),
            P("rep"),
            P(),
        ),
        out_specs=(P("rep", tp, None), P("rep", tp, None), P("rep", None), P("rep")),
        check_vma=False,
    )
```
